128 devices in a mesh: comp: 2 (over y_hi), gx: 16 (over x, z), gy: 4 (over y_lo, core).
Axes of the slice: x: 4, y: 4 (y_hi: 2, y_lo: 2; y = y_hi * 2 + y_lo), z: 4, core: 2. Of those that a mesh axis runs over, the one named last changes fastest.
Arguments:
- state: float32 [2, 16, 2048, 512], P('comp', None, 'gx', 'gy'), may hold values from -6 to 6
- diffusivity: float32 [2, 2048, 512], P('comp', 'gx', 'gy'), may hold values from 0.02 to 0.24
- mixing: float32 [2, 16, 2048, 512], P('comp', None, 'gx', 'gy'), may hold values from 0.1 to 4
- sea_mask: int32 [2048, 512], P('gx', 'gy'), may hold values 0 or 1
- source_row: int32 [2, 2048, 4, 2], P('comp', 'gx', 'gy'), may hold values from 0 to 2047, as said below
- regrid_weight: float32 [2, 2048, 2, 512, 128], P('comp', 'gx', None, 'gy'), may hold values from 0 to 1, as said below
Outputs:
- new_state: float32 [2, 16, 2048, 512], P('comp', None, 'gx', 'gy')
The draws below stay inside these ranges and needn't reach their ends.
Inputs may be any that keep to these rules, and one draw needn't show every extreme that they name: `source_row`: A source row lies in the other component at the same index along gy as its destination row. With a shift d drawn for each component and each index j along gy: atmosphere row x intersects ocean rows (x // 2 + k + d) mod 2048, ocean row x intersects atmosphere rows (2 x + k + d) mod 2048, for k < 2. regrid_weight[c, x, k, j * 128 + y, s] is zero unless s equals y or y + 1; the nonzero weights are positive, and for each destination cell they sum to 1 over k and s.
All inputs are finite; a program needn't handle non-finite values. No bound on the sum of `sea_mask` on one device may be relied on, other than what follows from the above.
Results may differ from the reference program's by a relative error of at most 0.0001.
Values sent between devices are 32-bit elements; how exact they have to be, the bound alone decides.
No kernel may reach another device: no remote copies, remote signals or barrier semaphores. Data moves between devices by JAX's collectives and lax.ppermute only.
A program may use at most 128 MiB of HBM per device.

```python
import math
import jax
import jax.numpy as jnp
from jax import lax

CX = 128
CY = 128
LEV = 16
F = 4
K = 2
SWEEPS = 4
NX = 2048
NY = 512
N_GY = 4


def draw_source_row(key, part):
    key = jax.random.fold_in(key, 11)
    shift = jax.random.randint(key, (2, 1, N_GY, 1), 0, 3 * CX, dtype=jnp.int32)
    rows = jnp.arange(NX, dtype=jnp.int32)[None, :, None, None]
    intersection = jnp.arange(K, dtype=jnp.int32)[None, None, None, :]
    which = jnp.arange(2, dtype=jnp.int32)[:, None, None, None]
    atmos_rows = (rows // 2 + intersection + shift) % NX
    ocean_rows = (2 * rows + intersection + shift) % NX
    return jnp.where(which == 0, atmos_rows, ocean_rows).astype(jnp.int32)


def draw_regrid_weight(key, part):
    key = jax.random.fold_in(key, 23)
    within = (jnp.arange(NY, dtype=jnp.int32) % CY)[None, None, None, :, None]
    source = jnp.arange(CY, dtype=jnp.int32)[None, None, None, None, :]
    band = ((source == within) | (source == within + 1)).astype(jnp.float32)
    raw = jax.random.uniform(key, (2, NX, K, NY, CY), jnp.float32, 0.5, 2.0) * band
    total = jnp.sum(raw, axis=(2, 4), keepdims=True)
    return (raw / total).astype(jnp.float32)


def set_ends(values, rng, smallest, largest):
    spot = [jax.random.randint(jax.random.fold_in(rng, axis), (), 0, length) for axis, length in enumerate(values.shape)]
    longest = values.shape.index(max(values.shape))
    beside = spot[:longest] + [(spot[longest] + 1) % values.shape[longest]] + spot[longest + 1:]
    return values.at[tuple(spot)].set(smallest).at[tuple(beside)].set(largest)


def steps_of(own_key, dims, pieces, least, largest):
    def one(dim, blocks):
        steps = jax.random.uniform(jax.random.fold_in(jax.random.fold_in(own_key, 6), dim), (blocks,), jnp.float32, least / len(pieces), largest / len(pieces))
        return jnp.repeat(jnp.exp(steps), dims[dim] // blocks).reshape((-1,) + (1,) * (len(dims) - dim - 1))

    factor_of = one(*pieces[0])
    for cut in pieces[1:]:
        factor_of = factor_of * one(*cut)
    return factor_of


def normal_values(key, shape, scale, most, shards=(), held_as=jnp.bfloat16):
    level = steps_of(key, shape, shards, -0.22, 0.18) if shards else 1.0
    values = jax.random.normal(key, shape, jnp.float32) * scale * level
    return jnp.minimum(jnp.maximum(values, -most), most).astype(held_as)


def setup_inputs(seed: int = 0) -> dict:
    key_of = jax.random.split(jax.random.key(seed), 7)
    state = normal_values(key_of[0], (2, LEV, NX, NY), 1.0, 6.0, ((0, 2), (2, 16), (3, 4)), jnp.float32)
    diffusivity = jnp.clip(jnp.exp(math.log(0.24) - 2.4849066 * jax.random.uniform(key_of[1], (2, NX, NY), jnp.float32) ** steps_of(key_of[1], (2, NX, NY), ((0, 2), (1, 16), (2, 4)), -0.2, 0.2)), 0.02, 0.24)
    mixing = jnp.clip(jnp.exp(math.log(4.0) - 3.6888794 * jax.random.uniform(key_of[2], (2, LEV, NX, NY), jnp.float32) ** steps_of(key_of[2], (2, LEV, NX, NY), ((0, 2), (2, 16), (3, 4)), -0.2, 0.2)), 0.1, 4.0)
    sea_mask = set_ends((jax.random.randint(key_of[3], (NX, NY), 0, 10) < 7).astype(jnp.int32), jax.random.fold_in(key_of[3], 1), 0, 1)
    source_row = draw_source_row(jax.random.fold_in(key_of[6], 71), 0)
    regrid_weight = draw_regrid_weight(jax.random.fold_in(key_of[6], 71), 0)
    return {"state": state, "diffusivity": diffusivity, "mixing": mixing, "sea_mask": sea_mask, "source_row": source_row, "regrid_weight": regrid_weight}


coupling = (0.8, 0.6, 0.4, 0.3)


def thomas(mixing_col, rhs_field):
    depth = rhs_field.shape[0]
    ratios = []
    partial_sol = []
    for layer_id in range(depth):
        if layer_id > 0:
            nu_below = mixing_col[layer_id - 1]
            diagonal = 1.0 + nu_below
        else:
            diagonal = jnp.ones_like(rhs_field[0])
        if layer_id < depth - 1:
            diagonal = diagonal + mixing_col[layer_id]
        if layer_id > 0:
            pivot = diagonal - nu_below * ratios[-1]
            value = (rhs_field[layer_id] + nu_below * partial_sol[-1]) / pivot
        else:
            pivot = diagonal
            value = rhs_field[0] / pivot
        if layer_id < depth - 1:
            ratios.append(mixing_col[layer_id] / pivot)
        else:
            ratios.append(jnp.zeros_like(pivot))
        partial_sol.append(value)
    result = [None] * depth
    result[depth - 1] = partial_sol[depth - 1]
    for layer_id in range(depth - 2, -1, -1):
        result[layer_id] = partial_sol[layer_id] + ratios[layer_id] * result[layer_id + 1]
    return jnp.stack(result)


def advance(padded, kappa, mixing_col, force_field, sea_field):
    centre = padded[:, 1:-1, 1:-1]
    lapl = padded[:, 2:, 1:-1] + padded[:, :-2, 1:-1] + padded[:, 1:-1, 2:] + padded[:, 1:-1, :-2] - 4.0 * centre
    rhs_field = centre + kappa * lapl + force_field
    solved = thomas(mixing_col, rhs_field)
    return jnp.where(sea_field > 0.5, solved, centre)


def regrid(rows_other, source_rows, weight_blocks):
    tiles = rows_other.reshape(F, NX, N_GY, CY)
    column_ids = jnp.arange(N_GY, dtype=jnp.int32)[None, :, None]
    picked = tiles[:, source_rows, column_ids, :]
    blocks = weight_blocks.reshape(NX, K, N_GY, CY, CY)
    merged = jnp.einsum('fxjks,xkjys->fxjy', picked, blocks, precision=lax.Precision.HIGHEST)
    return merged.reshape(F, NX, NY)


def reference(state, diffusivity, mixing, sea_mask, source_row, regrid_weight):
    surfaces = (state[0][::-1][:F], state[1][:F])
    sea_float = sea_mask.astype(jnp.float32)
    outputs = []
    for comp_id in range(2):
        other = regrid(surfaces[1 - comp_id], source_row[comp_id], regrid_weight[comp_id])
        total = jnp.zeros((NX, NY), jnp.float32)
        for level_id in range(F):
            total = total + coupling[level_id] * jnp.tanh(other[level_id])
        forcing = total - surfaces[comp_id][0]
        if comp_id == 1:
            sea_field = sea_float
        else:
            sea_field = jnp.ones_like(sea_float)
        forcing = forcing * sea_field
        target = LEV - 1 if comp_id == 0 else 0
        force_field = jnp.zeros_like(state[0]).at[target].set(forcing)
        field = state[comp_id]
        for sweep_id in range(SWEEPS):
            padded = jnp.pad(field, ((0, 0), (1, 1), (1, 1)))
            field = advance(padded, diffusivity[comp_id], mixing[comp_id], force_field, sea_field)
        outputs.append(field)
    return jnp.stack(outputs)
```

```python
import functools

import jax
import jax.numpy as jnp
from jax import lax
from jax.experimental import pallas as pl
from jax.experimental.pallas import tpu as pltpu
from jax.sharding import PartitionSpec as P

F = 4
SWEEPS = 4
LEV = 16
N = 128
HALO = 8
ROWS = N + 2 * HALO
GX = 16
UNIT = 64

coupling = (0.8, 0.6, 0.4, 0.3)

f32 = jnp.float32
VMEM = pl.BlockSpec(memory_space=pltpu.VMEM)
SMEM = pl.BlockSpec(memory_space=pltpu.SMEM)

PACK = (
    [(4 * q, 4) for q in range(LEV)]
    + [(64 + 3 * i, 3) for i in range(LEV - 1)]
    + [(109, 3), (112, 3)]
)


def params(vmem_mib):
    return pltpu.CompilerParams(vmem_limit_bytes=vmem_mib * 2**20)


def band_kernel(w_ref, out_ref):
    rows = w_ref.shape[0]
    sub = lax.broadcasted_iota(jnp.int32, (8, N), 0)
    lane = lax.broadcasted_iota(jnp.int32, (8, N), 1)
    same = sub == lane % 8
    after = sub == (lane + 7) % 8
    for k in range(2):
        own, nxt = [], []
        for x in range(rows):
            tile = w_ref[x, k, 0:8, :]
            for i in range(1, N // 8):
                tile = tile + w_ref[x, k, 8 * i : 8 * i + 8, :]
            own.append(jnp.sum(jnp.where(same, tile, 0.0), axis=0, keepdims=True))
            nxt.append(jnp.sum(jnp.where(after, tile, 0.0), axis=0, keepdims=True))
        out_ref[k] = jnp.concatenate(own, axis=0)
        out_ref[2 + k] = jnp.concatenate(nxt, axis=0)


def band(weight):
    step = 8
    return pl.pallas_call(
        band_kernel,
        grid=(N // step,),
        in_specs=[pl.BlockSpec((step, 2, N, N), lambda i: (i, 0, 0, 0))],
        out_specs=pl.BlockSpec((4, step, N), lambda i: (0, i, 0)),
        out_shape=jax.ShapeDtypeStruct((4, N, N), f32),
        compiler_params=params(56),
        cost_estimate=pl.CostEstimate(flops=2**22, bytes_accessed=2**24, transcendentals=0),
        name="band",
    )(weight)


def edge_kernel(par, state, mixing, kappa, mask, top, bottom):
    ocean = par[0] == 1
    for out, low in ((top, 0), (bottom, N - HALO)):
        rows = slice(low, low + HALO)
        sea = jnp.where(ocean, mask[rows].astype(f32), 1.0)
        for level in range(LEV):
            out[level] = state[level, rows]
        for level in range(LEV - 1):
            out[LEV + level] = mixing[level, rows] * sea
        out[2 * LEV - 1] = kappa[rows] * sea


def edges(par, state, mixing, kappa, mask):
    shape = jax.ShapeDtypeStruct((2 * LEV, HALO, N), f32)
    return pl.pallas_call(
        edge_kernel,
        in_specs=[SMEM] + [VMEM] * 4,
        out_specs=[VMEM, VMEM],
        out_shape=[shape, shape],
        compiler_params=params(16),
        name="edges",
    )(par, state, mixing, kappa, mask)


def force_kernel(par, a, b, c1, c2, diag, surf, mask, out, window, rows):
    comp, x, e, units = par[0], par[1], par[2], par[3]

    @pl.when(comp == 1)
    def _():
        odd = units % 2
        low = x < 8
        take_1 = low == (odd == 1)
        base = odd * UNIT
        at_a = pl.multiple_of(jnp.where(low, base, base + N), UNIT)
        at_b = pl.multiple_of(jnp.where(low, base + N, base), UNIT)
        at_c = pl.multiple_of((1 - odd) * 2 * N, UNIT)
        window[:, pl.ds(at_a, N), :] = a[...]
        window[:, pl.ds(at_b, N), :] = b[...]
        window[:, pl.ds(at_c, UNIT), :] = jnp.where(take_1, c1[...], c2[...])
        for f in range(F):
            for k in range(2):
                rows[k, f] = window[f, pl.ds(e + k, N, stride=2), :]

    @pl.when(comp == 0)
    def _():
        odd = (x + units) % 2

        @pl.when(odd == 0)
        def _():
            window[:, 0:N, :] = a[...]

        @pl.when(odd == 1)
        def _():
            window[:, 0:UNIT, :] = c1[...]
            window[:, UNIT:N, :] = c2[...]

        for f in range(F):
            for k in range(2):
                half = window[f, pl.ds(e + k, UNIT), :]
                rows[k, f, pl.ds(0, UNIT, stride=2), :] = half
                rows[k, f, pl.ds(1, UNIT, stride=2), :] = half

    total = jnp.zeros((N, N), f32)
    for i in range(F):
        scale = jnp.where(comp == 1, coupling[F - 1 - i], coupling[i])
        r0 = rows[0, i]
        r1 = rows[1, i]
        after = diag[2] * r0 + diag[3] * r1
        value = diag[0] * r0 + diag[1] * r1 + pltpu.roll(after, N - 1, 1)
        total = total + scale * jnp.tanh(value)
    own = surf[jnp.where(comp == 1, 0, F - 1)]
    sea = jnp.where(comp == 1, mask[...].astype(f32), 1.0)
    out[...] = (total - own) * sea


def force(par, pieces, diag, surf, mask):
    return pl.pallas_call(
        force_kernel,
        in_specs=[SMEM] + [VMEM] * 7,
        out_specs=VMEM,
        out_shape=jax.ShapeDtypeStruct((N, N), f32),
        scratch_shapes=[pltpu.VMEM((F, 5 * UNIT + 8, N), f32), pltpu.VMEM((2, F, N, N), f32)],
        compiler_params=params(16),
        name="force",
    )(par, *pieces, diag, surf, mask)


def column_kernel(par, state, mixing, kappa, mask, top, bottom, forcing, f_top, f_bottom, left, right, sea):
    ocean = par[0] == 1
    sea[...] = jnp.where(ocean, mask[...].astype(f32), 1.0)
    lane = lax.broadcasted_iota(jnp.int32, (8, N), 1)
    place = [(lane >= at) & (lane < at + width) for at, width in PACK]

    def tile(get):
        first = jnp.zeros((8, N), f32)
        last = jnp.zeros((8, N), f32)
        for q, (at, width) in enumerate(PACK):
            value = get(q)
            first = jnp.where(place[q], pltpu.roll(value, at, 1), first)
            last = jnp.where(place[q], pltpu.roll(value, (at + width) % N, 1), last)
        return first, last

    def ends(halo, f_halo, rows):
        left[rows], right[rows] = tile(lambda q: halo[q] if q < 2 * LEV else f_halo[...])

    ends(top, f_top, slice(0, HALO))
    ends(bottom, f_bottom, slice(HALO + N, ROWS))

    def body(t, carry):
        rows = pl.ds(pl.multiple_of(t * 8, 8), 8)
        s = sea[rows]

        def get(q):
            if q < LEV:
                return state[q, rows]
            if q < 2 * LEV - 1:
                return mixing[q - LEV, rows] * s
            if q < 2 * LEV:
                return kappa[rows] * s
            return forcing[rows]

        first, last = tile(get)
        out = pl.ds(pl.multiple_of(HALO + t * 8, 8), 8)
        left[out] = first
        right[out] = last
        return carry

    lax.fori_loop(0, N // 8, body, 0)


def columns(par, *arrays):
    shape = jax.ShapeDtypeStruct((ROWS, N), f32)
    return pl.pallas_call(
        column_kernel,
        in_specs=[SMEM] + [VMEM] * 9,
        out_specs=[VMEM, VMEM],
        out_shape=[shape, shape],
        scratch_shapes=[pltpu.VMEM((N, N), f32)],
        compiler_params=params(16),
        name="columns",
    )(par, *arrays)


PAD = ROWS + 16
BLOCK = 16


def sweep_kernel(
    par, state, mixing, kappa, mask, top, bottom, forcing, f_top, f_bottom, left, right, out,
    ua, ub, inv, below, above, kap, frc,
):
    ocean = par[0] == 1
    lane = lax.broadcasted_iota(jnp.int32, (8, N), 1)
    zero = jnp.zeros((8, 2 * N), f32)
    for u in (ua, ub):
        for level in range(LEV):
            u[level, 0:8] = zero
            u[level, PAD - 8 : PAD] = zero

    def setup(get, package_rows, rows):
        pl_ = left[package_rows]
        pr = right[package_rows]

        def field(q):
            at, width = PACK[q]
            after = pltpu.roll(pl_, (N - at) % N, 1)
            before = pltpu.roll(pr, (2 * N - at - width) % N, 1)
            side = jnp.where(lane < width, after, jnp.where(lane >= N - width, before, 0.0))
            return jnp.concatenate([get(q), side], axis=1)

        for level in range(LEV):
            ua[level, rows] = field(level)
        kap[rows] = field(2 * LEV - 1)
        frc[rows] = field(2 * LEV)
        nu_before = None
        ratio = None
        for level in range(LEV):
            pivot = jnp.ones((8, 2 * N), f32)
            if level > 0:
                pivot = pivot + nu_before
            if level < LEV - 1:
                nu = field(LEV + level)
                pivot = pivot + nu
            if level > 0:
                pivot = pivot - nu_before * ratio
            r = 1.0 / pivot
            inv[level, rows] = r
            if level > 0:
                below[level, rows] = nu_before * r
            if level < LEV - 1:
                ratio = nu * r
                above[level, rows] = ratio
                nu_before = nu

    def ends(halo, f_halo, package_rows, rows):
        setup(lambda q: halo[q] if q < 2 * LEV else f_halo[...], package_rows, rows)

    ends(top, f_top, slice(0, 8), slice(8, 16))
    ends(bottom, f_bottom, slice(HALO + N, ROWS), slice(HALO + N + 8, ROWS + 8))

    def build(t, carry):
        src = pl.ds(pl.multiple_of(t * 8, 8), 8)
        s = jnp.where(ocean, mask[src].astype(f32), 1.0)

        def get(q):
            if q < LEV:
                return state[q, src]
            if q < 2 * LEV - 1:
                return mixing[q - LEV, src] * s
            if q < 2 * LEV:
                return kappa[src] * s
            return forcing[src]

        setup(
            get,
            pl.ds(pl.multiple_of(HALO + t * 8, 8), 8),
            pl.ds(pl.multiple_of(HALO + 8 + t * 8, 8), 8),
        )
        return carry

    lax.fori_loop(0, N // 8, build, 0)

    top_force = jnp.where(ocean, 1.0, 0.0)
    bottom_force = jnp.where(ocean, 0.0, 1.0)
    first_row = lax.broadcasted_iota(jnp.int32, (8, 2 * N), 0) == 0
    last_row = lax.broadcasted_iota(jnp.int32, (8, 2 * N), 0) == 7

    def solve(u, base, store):
        tiles = range(BLOCK // 8)
        rows = [pl.ds(pl.multiple_of(base + 8 * i, 8), 8) for i in tiles]
        before = pl.ds(pl.multiple_of(base - 8, 8), 8)
        behind = pl.ds(pl.multiple_of(base + BLOCK, 8), 8)
        k = [kap[r] for r in rows]
        keep = [1.0 - 4.0 * x for x in k]
        part = []
        for level in range(LEV):
            c = [u[level, r] for r in rows]
            around = [u[level, before]] + c + [u[level, behind]]
            row = []
            for i in tiles:
                up = pltpu.roll(jnp.where(last_row, around[i], c[i]), 1, 0)
                down = pltpu.roll(jnp.where(first_row, around[i + 2], c[i]), 7, 0)
                sides = pltpu.roll(c[i], 1, 1) + pltpu.roll(c[i], 2 * N - 1, 1)
                rhs = keep[i] * c[i] + k[i] * ((up + down) + sides)
                if level == 0:
                    rhs = rhs + top_force * frc[rows[i]]
                if level == LEV - 1:
                    rhs = rhs + bottom_force * frc[rows[i]]
                value = rhs * inv[level, rows[i]]
                if level > 0:
                    value = value + below[level, rows[i]] * part[-1][i]
                row.append(value)
            part.append(row)
        v = part[LEV - 1]
        for i in tiles:
            store(LEV - 1, i, v[i])
        for level in range(LEV - 2, -1, -1):
            v = [part[level][i] + above[level, rows[i]] * v[i] for i in tiles]
            for i in tiles:
                store(level, i, v[i])

    for s in range(SWEEPS):
        src, dst = (ua, ub) if s % 2 == 0 else (ub, ua)
        if s < SWEEPS - 1:

            def body(t, carry, src=src, dst=dst):
                base = pl.multiple_of(t * BLOCK + 8, 8)

                def store(level, i, v):
                    dst[level, pl.ds(pl.multiple_of(base + 8 * i, 8), 8)] = v

                solve(src, base, store)
                return carry

            lax.fori_loop(0, ROWS // BLOCK, body, 0)
        else:

            def body(t, carry, src=src):
                base = pl.multiple_of(t * BLOCK + 16, 8)
                o = pl.multiple_of(t * BLOCK, 8)

                def store(level, i, v):
                    out[level, pl.ds(pl.multiple_of(o + 8 * i, 8), 8)] = v[:, :N]

                solve(src, base, store)
                return carry

            lax.fori_loop(0, N // BLOCK, body, 0)


def sweeps(par, *arrays):
    wide = pltpu.VMEM((LEV, PAD, 2 * N), f32)
    return pl.pallas_call(
        sweep_kernel,
        in_specs=[SMEM] + [VMEM] * 11,
        out_specs=VMEM,
        out_shape=jax.ShapeDtypeStruct((LEV, N, N), f32),
        scratch_shapes=[wide] * 5 + [pltpu.VMEM((PAD, 2 * N), f32)] * 2,
        compiler_params=params(40),
        name="sweeps",
    )(par, *arrays)


def shift_pair(low_edge, high_edge, axis):
    count = lax.axis_size(axis)
    up = [(i, i + 1) for i in range(count - 1)]
    down = [(i + 1, i) for i in range(count - 1)]
    return lax.ppermute(high_edge, axis, up), lax.ppermute(low_edge, axis, down)


BOTH = ("comp", "gx")


def routed(block, route):
    route = route % 32
    pairs = [
        (GX + (2 * x + route % GX + ((x >= 8) != (route >= GX))) % GX, GX + x) for x in range(GX)
    ]
    pairs += [((x + route) // 2 % GX, x) for x in range(GX) if (x + route) % 2 == 0]
    return lax.ppermute(block, BOTH, pairs)


def ocean_route(units):
    base = units // 2
    odd = units % 2

    def run(peer):
        whole = (base + odd) % GX
        part = (base + 1 - odd) % GX
        half = peer[:, UNIT:] if odd else peer[:, :UNIT]
        return (
            routed(peer, whole),
            routed(peer, GX + whole),
            routed(half, part),
            routed(half, GX + part),
        )

    return run


def atmosphere_route(units):
    def run(peer):
        return (
            routed(peer, units),
            peer,
            routed(peer[:, UNIT:], units - 1),
            routed(peer[:, :UNIT], units + 1),
        )

    return run


def shards(state, diffusivity, mixing, sea_mask, source_row, regrid_weight):
    comp = lax.axis_index("comp")
    gx = lax.axis_index("gx")
    field = state[0]
    mix = mixing[0]
    kappa = diffusivity[0]
    surf = lax.dynamic_slice(field, ((LEV - F) * (1 - comp), 0, 0), (F, N, N))
    swap = [(x, GX + x) for x in range(GX)] + [(GX + x, x) for x in range(GX)]
    peer = lax.ppermute(surf, BOTH, swap)
    first = source_row[0, 0, 0, 0]
    units = jnp.where(comp == 1, first // UNIT - 4 * gx, first // UNIT - gx) % 32
    par = jnp.stack([comp, gx, first % UNIT, units]).astype(jnp.int32)
    diag = band(regrid_weight[0])
    top, bottom = shift_pair(*edges(par, field, mix, kappa, sea_mask), "gx")
    peer, diag, top, bottom = lax.optimization_barrier((peer, diag, top, bottom))
    pieces = lax.switch(
        comp * 32 + units,
        [atmosphere_route(i) for i in range(32)] + [ocean_route(i) for i in range(32)],
        peer,
    )
    forcing = force(par, pieces, diag, surf, sea_mask)
    f_top, f_bottom = shift_pair(forcing[:HALO], forcing[N - HALO :], "gx")
    own = (field, mix, kappa, sea_mask, top, bottom, forcing, f_top, f_bottom)
    first_columns, last_columns = columns(par, *own)
    before, after = shift_pair(first_columns, last_columns, "gy")
    return sweeps(par, *own, after, before)[None]


def solution(mesh):
    placed = (
        P("comp", None, "gx", "gy"),
        P("comp", "gx", "gy"),
        P("comp", None, "gx", "gy"),
        P("gx", "gy"),
        P("comp", "gx", "gy", None),
        P("comp", "gx", None, "gy", None),
    )
    return jax.shard_map(
        shards, mesh=mesh, in_specs=placed, out_specs=P("comp", None, "gx", "gy"), check_vma=False
    )
```

```python
import functools

import jax
import jax.numpy as jnp
from jax import lax
from jax.experimental import pallas as pl
from jax.experimental.pallas import tpu as pltpu
from jax.sharding import PartitionSpec as P

F = 4
SWEEPS = 4
LEV = 16
N = 128
HALO = 8
ROWS = N + 2 * HALO
GX = 16
UNIT = 64

coupling = (0.8, 0.6, 0.4, 0.3)

f32 = jnp.float32
VMEM = pl.BlockSpec(memory_space=pltpu.VMEM)
SMEM = pl.BlockSpec(memory_space=pltpu.SMEM)

PACK = (
    [(4 * q, 4) for q in range(LEV)]
    + [(64 + 3 * i, 3) for i in range(LEV - 1)]
    + [(109, 3), (112, 3)]
)


def params(vmem_mib):
    return pltpu.CompilerParams(vmem_limit_bytes=vmem_mib * 2**20)


CHUNKS = 16


def band_kernel(w_hbm, out_ref, w_ref, sems):
    rows = N // CHUNKS

    def copy(i):
        at = pl.ds(i * rows, rows)
        return pltpu.make_async_copy(w_hbm.at[at], w_ref.at[at], sems.at[i])

    for i in range(CHUNKS):
        copy(i).start()
    sub = lax.broadcasted_iota(jnp.int32, (8, N), 0)
    lane = lax.broadcasted_iota(jnp.int32, (8, N), 1)
    same = sub == lane % 8
    after = sub == (lane + 7) % 8

    def body(i, carry):
        copy(i).wait()
        base = pl.multiple_of(i * rows, rows)
        for k in range(2):
            own, nxt = [], []
            for x in range(rows):
                tile = w_ref[base + x, k, 0:8, :]
                for t in range(1, N // 8):
                    tile = tile + w_ref[base + x, k, 8 * t : 8 * t + 8, :]
                own.append(jnp.sum(jnp.where(same, tile, 0.0), axis=0, keepdims=True))
                nxt.append(jnp.sum(jnp.where(after, tile, 0.0), axis=0, keepdims=True))
            out_ref[k, pl.ds(base, rows)] = jnp.concatenate(own, axis=0)
            out_ref[2 + k, pl.ds(base, rows)] = jnp.concatenate(nxt, axis=0)
        return carry

    lax.fori_loop(0, CHUNKS, body, 0)


def band(weight):
    return pl.pallas_call(
        band_kernel,
        in_specs=[pl.BlockSpec(memory_space=pl.ANY)],
        out_specs=VMEM,
        out_shape=jax.ShapeDtypeStruct((4, N, N), f32),
        scratch_shapes=[pltpu.VMEM((N, 2, N, N), f32), pltpu.SemaphoreType.DMA((CHUNKS,))],
        compiler_params=params(48),
        cost_estimate=pl.CostEstimate(flops=2**22, bytes_accessed=2**24, transcendentals=0),
        name="band",
    )(weight)


def edge_kernel(
    where, source, state, mixing, kappa, mask, top, bottom, par, choice, s_ref, m_ref, k_ref, i_ref, sems
):
    comp, x = where[0], where[1]
    copies = []
    for side, low in enumerate((0, N - HALO)):
        rows = pl.ds(low, HALO)
        for n, (src, dst) in enumerate(
            (
                (state.at[:, rows], s_ref.at[side]),
                (mixing.at[:, rows], m_ref.at[side]),
                (kappa.at[rows], k_ref.at[side]),
                (mask.at[rows], i_ref.at[side]),
            )
        ):
            copies.append(pltpu.make_async_copy(src, dst, sems.at[4 * side + n]))
    for c in copies:
        c.start()
    first = source[0, 0]
    units = lax.rem(first // UNIT + 128 - jnp.where(comp == 1, 4, 1) * x, 32)
    par[0] = comp
    par[1] = x
    par[2] = lax.rem(first, UNIT)
    par[3] = units
    choice[0] = comp * 32 + units
    for c in copies:
        c.wait()
    for side, out in enumerate((top, bottom)):
        sea = jnp.where(comp == 1, i_ref[side].astype(f32), 1.0)
        for level in range(LEV):
            out[level] = s_ref[side, level]
        for level in range(LEV - 1):
            out[LEV + level] = m_ref[side, level] * sea
        out[2 * LEV - 1] = k_ref[side] * sea


def edges(where, source, state, mixing, kappa, mask):
    shape = jax.ShapeDtypeStruct((2 * LEV, HALO, N), f32)
    hbm = pl.BlockSpec(memory_space=pl.ANY)
    return pl.pallas_call(
        edge_kernel,
        in_specs=[SMEM, SMEM] + [hbm] * 4,
        out_specs=[VMEM, VMEM, SMEM, SMEM],
        out_shape=[
            shape,
            shape,
            jax.ShapeDtypeStruct((4,), jnp.int32),
            jax.ShapeDtypeStruct((1,), jnp.int32),
        ],
        scratch_shapes=[
            pltpu.VMEM((2, LEV, HALO, N), f32),
            pltpu.VMEM((2, LEV, HALO, N), f32),
            pltpu.VMEM((2, HALO, N), f32),
            pltpu.VMEM((2, HALO, N), jnp.int32),
            pltpu.SemaphoreType.DMA((8,)),
        ],
        compiler_params=params(60),
        name="edges",
    )(where, source, state, mixing, kappa, mask)


def force_kernel(par, a, b, c1, c2, diag, surf, mask, out, window, rows):
    comp, x, e, units = par[0], par[1], par[2], par[3]

    @pl.when(comp == 1)
    def _():
        odd = units % 2
        low = x < 8
        take_1 = low == (odd == 1)
        base = odd * UNIT
        at_a = pl.multiple_of(jnp.where(low, base, base + N), UNIT)
        at_b = pl.multiple_of(jnp.where(low, base + N, base), UNIT)
        at_c = pl.multiple_of((1 - odd) * 2 * N, UNIT)
        window[:, pl.ds(at_a, N), :] = a[...]
        window[:, pl.ds(at_b, N), :] = b[...]
        window[:, pl.ds(at_c, UNIT), :] = jnp.where(take_1, c1[...], c2[...])
        for f in range(F):
            for k in range(2):
                rows[k, f] = window[f, pl.ds(e + k, N, stride=2), :]

    @pl.when(comp == 0)
    def _():
        odd = (x + units) % 2

        @pl.when(odd == 0)
        def _():
            window[:, 0:N, :] = a[...]

        @pl.when(odd == 1)
        def _():
            window[:, 0:UNIT, :] = c1[...]
            window[:, UNIT:N, :] = c2[...]

        for f in range(F):
            for k in range(2):
                half = window[f, pl.ds(e + k, UNIT), :]
                rows[k, f, pl.ds(0, UNIT, stride=2), :] = half
                rows[k, f, pl.ds(1, UNIT, stride=2), :] = half

    total = jnp.zeros((N, N), f32)
    for i in range(F):
        scale = jnp.where(comp == 1, coupling[F - 1 - i], coupling[i])
        r0 = rows[0, i]
        r1 = rows[1, i]
        after = diag[2] * r0 + diag[3] * r1
        value = diag[0] * r0 + diag[1] * r1 + pltpu.roll(after, N - 1, 1)
        total = total + scale * jnp.tanh(value)
    own = surf[jnp.where(comp == 1, 0, F - 1)]
    sea = jnp.where(comp == 1, mask[...].astype(f32), 1.0)
    out[...] = (total - own) * sea


def force(par, pieces, diag, surf, mask):
    return pl.pallas_call(
        force_kernel,
        in_specs=[SMEM] + [VMEM] * 7,
        out_specs=VMEM,
        out_shape=jax.ShapeDtypeStruct((N, N), f32),
        scratch_shapes=[pltpu.VMEM((F, 5 * UNIT + 8, N), f32), pltpu.VMEM((2, F, N, N), f32)],
        compiler_params=params(16),
        name="force",
    )(par, *pieces, diag, surf, mask)


def column_kernel(par, state, mixing, kappa, mask, top, bottom, forcing, f_top, f_bottom, left, right, sea):
    ocean = par[0] == 1
    sea[...] = jnp.where(ocean, mask[...].astype(f32), 1.0)
    lane = lax.broadcasted_iota(jnp.int32, (8, N), 1)
    place = [(lane >= at) & (lane < at + width) for at, width in PACK]

    def tile(get):
        first = jnp.zeros((8, N), f32)
        last = jnp.zeros((8, N), f32)
        for q, (at, width) in enumerate(PACK):
            value = get(q)
            first = jnp.where(place[q], pltpu.roll(value, at, 1), first)
            last = jnp.where(place[q], pltpu.roll(value, (at + width) % N, 1), last)
        return first, last

    def ends(halo, f_halo, rows):
        left[rows], right[rows] = tile(lambda q: halo[q] if q < 2 * LEV else f_halo[...])

    ends(top, f_top, slice(0, HALO))
    ends(bottom, f_bottom, slice(HALO + N, ROWS))

    def body(t, carry):
        rows = pl.ds(pl.multiple_of(t * 8, 8), 8)
        s = sea[rows]

        def get(q):
            if q < LEV:
                return state[q, rows]
            if q < 2 * LEV - 1:
                return mixing[q - LEV, rows] * s
            if q < 2 * LEV:
                return kappa[rows] * s
            return forcing[rows]

        first, last = tile(get)
        out = pl.ds(pl.multiple_of(HALO + t * 8, 8), 8)
        left[out] = first
        right[out] = last
        return carry

    lax.fori_loop(0, N // 8, body, 0)


def columns(par, *arrays):
    shape = jax.ShapeDtypeStruct((ROWS, N), f32)
    return pl.pallas_call(
        column_kernel,
        in_specs=[SMEM] + [VMEM] * 9,
        out_specs=[VMEM, VMEM],
        out_shape=[shape, shape],
        scratch_shapes=[pltpu.VMEM((N, N), f32)],
        compiler_params=params(16),
        name="columns",
    )(par, *arrays)


PAD = ROWS + 16
BLOCK = 16


def sweep_kernel(
    par, state, mixing, kappa, mask, top, bottom, forcing, f_top, f_bottom, left, right, out,
    ua, ub, inv, below, above, kap, frc,
):
    ocean = par[0] == 1
    lane = lax.broadcasted_iota(jnp.int32, (8, N), 1)
    zero = jnp.zeros((8, 2 * N), f32)
    for u in (ua, ub):
        for level in range(LEV):
            u[level, 0:8] = zero
            u[level, PAD - 8 : PAD] = zero

    def setup(get, package_rows, rows):
        pl_ = left[package_rows]
        pr = right[package_rows]

        def field(q):
            at, width = PACK[q]
            after = pltpu.roll(pl_, (N - at) % N, 1)
            before = pltpu.roll(pr, (2 * N - at - width) % N, 1)
            side = jnp.where(lane < width, after, jnp.where(lane >= N - width, before, 0.0))
            return jnp.concatenate([get(q), side], axis=1)

        for level in range(LEV):
            ua[level, rows] = field(level)
        kap[rows] = field(2 * LEV - 1)
        frc[rows] = field(2 * LEV)
        nu_before = None
        ratio = None
        for level in range(LEV):
            pivot = jnp.ones((8, 2 * N), f32)
            if level > 0:
                pivot = pivot + nu_before
            if level < LEV - 1:
                nu = field(LEV + level)
                pivot = pivot + nu
            if level > 0:
                pivot = pivot - nu_before * ratio
            r = 1.0 / pivot
            inv[level, rows] = r
            if level > 0:
                below[level, rows] = nu_before * r
            if level < LEV - 1:
                ratio = nu * r
                above[level, rows] = ratio
                nu_before = nu

    def ends(halo, f_halo, package_rows, rows):
        setup(lambda q: halo[q] if q < 2 * LEV else f_halo[...], package_rows, rows)

    ends(top, f_top, slice(0, 8), slice(8, 16))
    ends(bottom, f_bottom, slice(HALO + N, ROWS), slice(HALO + N + 8, ROWS + 8))

    def build(t, carry):
        src = pl.ds(pl.multiple_of(t * 8, 8), 8)
        s = jnp.where(ocean, mask[src].astype(f32), 1.0)

        def get(q):
            if q < LEV:
                return state[q, src]
            if q < 2 * LEV - 1:
                return mixing[q - LEV, src] * s
            if q < 2 * LEV:
                return kappa[src] * s
            return forcing[src]

        setup(
            get,
            pl.ds(pl.multiple_of(HALO + t * 8, 8), 8),
            pl.ds(pl.multiple_of(HALO + 8 + t * 8, 8), 8),
        )
        return carry

    lax.fori_loop(0, N // 8, build, 0)

    top_force = jnp.where(ocean, 1.0, 0.0)
    bottom_force = jnp.where(ocean, 0.0, 1.0)
    first_row = lax.broadcasted_iota(jnp.int32, (8, 2 * N), 0) == 0
    last_row = lax.broadcasted_iota(jnp.int32, (8, 2 * N), 0) == 7

    def solve(u, base, store):
        tiles = range(BLOCK // 8)
        rows = [pl.ds(pl.multiple_of(base + 8 * i, 8), 8) for i in tiles]
        before = pl.ds(pl.multiple_of(base - 8, 8), 8)
        behind = pl.ds(pl.multiple_of(base + BLOCK, 8), 8)
        k = [kap[r] for r in rows]
        keep = [1.0 - 4.0 * x for x in k]
        part = []
        for level in range(LEV):
            c = [u[level, r] for r in rows]
            around = [u[level, before]] + c + [u[level, behind]]
            row = []
            for i in tiles:
                up = pltpu.roll(jnp.where(last_row, around[i], c[i]), 1, 0)
                down = pltpu.roll(jnp.where(first_row, around[i + 2], c[i]), 7, 0)
                sides = pltpu.roll(c[i], 1, 1) + pltpu.roll(c[i], 2 * N - 1, 1)
                rhs = keep[i] * c[i] + k[i] * ((up + down) + sides)
                if level == 0:
                    rhs = rhs + top_force * frc[rows[i]]
                if level == LEV - 1:
                    rhs = rhs + bottom_force * frc[rows[i]]
                value = rhs * inv[level, rows[i]]
                if level > 0:
                    value = value + below[level, rows[i]] * part[-1][i]
                row.append(value)
            part.append(row)
        v = part[LEV - 1]
        for i in tiles:
            store(LEV - 1, i, v[i])
        for level in range(LEV - 2, -1, -1):
            v = [part[level][i] + above[level, rows[i]] * v[i] for i in tiles]
            for i in tiles:
                store(level, i, v[i])

    for s in range(SWEEPS):
        src, dst = (ua, ub) if s % 2 == 0 else (ub, ua)
        if s < SWEEPS - 1:

            def body(t, carry, src=src, dst=dst):
                base = pl.multiple_of(t * BLOCK + 8, 8)

                def store(level, i, v):
                    dst[level, pl.ds(pl.multiple_of(base + 8 * i, 8), 8)] = v

                solve(src, base, store)
                return carry

            lax.fori_loop(0, ROWS // BLOCK, body, 0)
        else:

            def body(t, carry, src=src):
                base = pl.multiple_of(t * BLOCK + 16, 8)
                o = pl.multiple_of(t * BLOCK, 8)

                def store(level, i, v):
                    out[level, pl.ds(pl.multiple_of(o + 8 * i, 8), 8)] = v[:, :N]

                solve(src, base, store)
                return carry

            lax.fori_loop(0, N // BLOCK, body, 0)


def sweeps(par, *arrays):
    wide = pltpu.VMEM((LEV, PAD, 2 * N), f32)
    return pl.pallas_call(
        sweep_kernel,
        in_specs=[SMEM] + [VMEM] * 11,
        out_specs=VMEM,
        out_shape=jax.ShapeDtypeStruct((LEV, N, N), f32),
        scratch_shapes=[wide] * 5 + [pltpu.VMEM((PAD, 2 * N), f32)] * 2,
        compiler_params=params(40),
        name="sweeps",
    )(par, *arrays)


def shift_pair(low_edge, high_edge, axis):
    count = lax.axis_size(axis)
    up = [(i, i + 1) for i in range(count - 1)]
    down = [(i + 1, i) for i in range(count - 1)]
    return lax.ppermute(high_edge, axis, up), lax.ppermute(low_edge, axis, down)


BOTH = ("comp", "gx")


MERGED = 16


def ocean_pairs(route):
    return [
        (GX + (2 * x + route % GX + ((x >= 8) != (route >= GX))) % GX, GX + x) for x in range(GX)
    ]


def atmosphere_pairs(route):
    return [((x + route) // 2 % GX, x) for x in range(GX) if (x + route) % 2 == 0]


def listed(block, entry):
    pairs = ocean_pairs((entry + 15) % 32) + atmosphere_pairs(entry)
    if entry == MERGED + 15:
        pairs += atmosphere_pairs(MERGED)
    return lax.ppermute(block, BOTH, pairs)


def atmosphere_routed(block, route):
    route = route % 32
    return listed(block, route if route != MERGED else MERGED + 15)


def ocean_route(units):
    base = units // 2
    odd = units % 2

    def run(peer):
        whole = (base + odd) % GX
        part = (base + 1 - odd) % GX
        half = peer[:, UNIT:] if odd else peer[:, :UNIT]
        jobs = [(peer, whole), (peer, GX + whole), (half, part), (half, GX + part)]
        entries = [(route + 17) % 32 for _, route in jobs]
        if MERGED not in entries:
            return tuple(listed(block, entry) for (block, _), entry in zip(jobs, entries))
        results = []
        last = peer[:1, :8]

        def chained(block, entry):
            nonlocal last
            block, _ = lax.optimization_barrier((block, last))
            last = listed(block, entry)
            return last

        for (block, _), entry in zip(jobs, entries):
            if entry != MERGED:
                results.append(chained(block, entry))
            else:
                low, high = chained(block, 17), chained(block, 31)
                results.append(jnp.where(lax.axis_index("gx") < 8, low, high))
        return tuple(results)

    return run


def atmosphere_route(units):
    def run(peer):
        return (
            atmosphere_routed(peer, units),
            peer,
            atmosphere_routed(peer[:, UNIT:], units - 1),
            atmosphere_routed(peer[:, :UNIT], units + 1),
        )

    return run


def shards(state, diffusivity, mixing, sea_mask, source_row, regrid_weight):
    comp = lax.axis_index("comp")
    gx = lax.axis_index("gx")
    field = state[0]
    mix = mixing[0]
    kappa = diffusivity[0]
    surf = lax.dynamic_slice(field, ((LEV - F) * (1 - comp), 0, 0), (F, N, N))
    swap = [(x, GX + x) for x in range(GX)] + [(GX + x, x) for x in range(GX)]
    peer = lax.ppermute(surf, BOTH, swap)
    where = jnp.stack([comp, gx]).astype(jnp.int32)
    source = jnp.transpose(source_row[0, :, 0, :])
    low, high, par, choice = edges(where, source, field, mix, kappa, sea_mask)
    diag = band(regrid_weight[0])
    top, bottom = shift_pair(low, high, "gx")
    peer, diag, top, bottom = lax.optimization_barrier((peer, diag, top, bottom))
    pieces = lax.switch(
        choice[0],
        [atmosphere_route(i) for i in range(32)] + [ocean_route(i) for i in range(32)],
        peer,
    )
    forcing = force(par, pieces, diag, surf, sea_mask)
    f_top, f_bottom = shift_pair(forcing[:HALO], forcing[N - HALO :], "gx")
    own = (field, mix, kappa, sea_mask, top, bottom, forcing, f_top, f_bottom)
    first_columns, last_columns = columns(par, *own)
    before, after = shift_pair(first_columns, last_columns, "gy")
    return sweeps(par, *own, after, before)[None]


def solution(mesh):
    placed = (
        P("comp", None, "gx", "gy"),
        P("comp", "gx", "gy"),
        P("comp", None, "gx", "gy"),
        P("gx", "gy"),
        P("comp", "gx", "gy", None),
        P("comp", "gx", None, "gy", None),
    )
    return jax.shard_map(
        shards, mesh=mesh, in_specs=placed, out_specs=P("comp", None, "gx", "gy"), check_vma=False
    )
```

```python
import functools

import jax
import jax.numpy as jnp
from jax import lax
from jax.experimental import pallas as pl
from jax.experimental.pallas import tpu as pltpu
from jax.sharding import PartitionSpec as P

F = 4
SWEEPS = 4
LEV = 16
N = 128
HALO = 8
ROWS = N + 2 * HALO
GX = 16
UNIT = 64

coupling = (0.8, 0.6, 0.4, 0.3)

f32 = jnp.float32
VMEM = pl.BlockSpec(memory_space=pltpu.VMEM)
SMEM = pl.BlockSpec(memory_space=pltpu.SMEM)

PACK = (
    [(4 * q, 4) for q in range(LEV)]
    + [(64 + 3 * i, 3) for i in range(LEV - 1)]
    + [(109, 3), (112, 3)]
)


def params(vmem_mib):
    return pltpu.CompilerParams(vmem_limit_bytes=vmem_mib * 2**20)


CHUNKS = 16


def band_kernel(w_hbm, out_ref, w_ref, sems):
    rows = N // CHUNKS

    def copy(i):
        at = pl.ds(i * rows, rows)
        return pltpu.make_async_copy(w_hbm.at[at], w_ref.at[at], sems.at[i])

    for i in range(CHUNKS):
        copy(i).start()
    sub = lax.broadcasted_iota(jnp.int32, (8, N), 0)
    lane = lax.broadcasted_iota(jnp.int32, (8, N), 1)
    same = sub == lane % 8
    after = sub == (lane + 7) % 8

    def body(i, carry):
        copy(i).wait()
        base = pl.multiple_of(i * rows, rows)
        for k in range(2):
            own, nxt = [], []
            for x in range(rows):
                tile = w_ref[base + x, k, 0:8, :]
                for t in range(1, N // 8):
                    tile = tile + w_ref[base + x, k, 8 * t : 8 * t + 8, :]
                own.append(jnp.sum(jnp.where(same, tile, 0.0), axis=0, keepdims=True))
                nxt.append(jnp.sum(jnp.where(after, tile, 0.0), axis=0, keepdims=True))
            out_ref[k, pl.ds(base, rows)] = jnp.concatenate(own, axis=0)
            out_ref[2 + k, pl.ds(base, rows)] = jnp.concatenate(nxt, axis=0)
        return carry

    lax.fori_loop(0, CHUNKS, body, 0)


def band(weight):
    return pl.pallas_call(
        band_kernel,
        in_specs=[pl.BlockSpec(memory_space=pl.ANY)],
        out_specs=VMEM,
        out_shape=jax.ShapeDtypeStruct((4, N, N), f32),
        scratch_shapes=[pltpu.VMEM((N, 2, N, N), f32), pltpu.SemaphoreType.DMA((CHUNKS,))],
        compiler_params=params(48),
        cost_estimate=pl.CostEstimate(flops=2**22, bytes_accessed=2**24, transcendentals=0),
        name="band",
    )(weight)


def shift_kernel(where, source, par, choice):
    comp, x = where[0], where[1]
    first = source[0, 0]
    units = lax.rem(first // UNIT + 128 - jnp.where(comp == 1, 4, 1) * x, 32)
    par[0] = comp
    par[1] = x
    par[2] = lax.rem(first, UNIT)
    par[3] = units
    choice[0] = comp * 32 + units


def shift(where, source):
    return pl.pallas_call(
        shift_kernel,
        in_specs=[SMEM, SMEM],
        out_specs=[SMEM, SMEM],
        out_shape=[jax.ShapeDtypeStruct((4,), jnp.int32), jax.ShapeDtypeStruct((1,), jnp.int32)],
        name="shift",
    )(where, source)


def force_kernel(
    par, a, b, c1, c2, diag, surf, mask, state, mixing, kappa, out, first, last,
    window, rows, m_ref, k_ref, sems,
):
    comp, x, e, units = par[0], par[1], par[2], par[3]
    copies = []
    for side, (edge, low) in enumerate(((first, 0), (last, N - HALO))):
        at = pl.ds(low, HALO)
        for n, (src, dst) in enumerate(
            (
                (state.at[:, at], edge.at[pl.ds(0, LEV)]),
                (mixing.at[:, at], m_ref.at[side]),
                (kappa.at[at], k_ref.at[side]),
            )
        ):
            copies.append(pltpu.make_async_copy(src, dst, sems.at[3 * side + n]))
    for copy in copies:
        copy.start()

    @pl.when(comp == 1)
    def _():
        odd = units % 2
        low = x < 8
        take_1 = low == (odd == 1)
        base = odd * UNIT
        at_a = pl.multiple_of(jnp.where(low, base, base + N), UNIT)
        at_b = pl.multiple_of(jnp.where(low, base + N, base), UNIT)
        at_c = pl.multiple_of((1 - odd) * 2 * N, UNIT)
        window[:, pl.ds(at_a, N), :] = a[...]
        window[:, pl.ds(at_b, N), :] = b[...]
        window[:, pl.ds(at_c, UNIT), :] = jnp.where(take_1, c1[...], c2[...])
        for f in range(F):
            for k in range(2):
                rows[k, f] = window[f, pl.ds(e + k, N, stride=2), :]

    @pl.when(comp == 0)
    def _():
        odd = (x + units) % 2

        @pl.when(odd == 0)
        def _():
            window[:, 0:N, :] = a[...]

        @pl.when(odd == 1)
        def _():
            window[:, 0:UNIT, :] = c1[...]
            window[:, UNIT:N, :] = c2[...]

        for f in range(F):
            for k in range(2):
                half = window[f, pl.ds(e + k, UNIT), :]
                rows[k, f, pl.ds(0, UNIT, stride=2), :] = half
                rows[k, f, pl.ds(1, UNIT, stride=2), :] = half

    total = jnp.zeros((N, N), f32)
    for i in range(F):
        scale = jnp.where(comp == 1, coupling[F - 1 - i], coupling[i])
        r0 = rows[0, i]
        r1 = rows[1, i]
        after = diag[2] * r0 + diag[3] * r1
        value = diag[0] * r0 + diag[1] * r1 + pltpu.roll(after, N - 1, 1)
        total = total + scale * jnp.tanh(value)
    own = surf[jnp.where(comp == 1, 0, F - 1)]
    sea = jnp.where(comp == 1, mask[...].astype(f32), 1.0)
    forcing = (total - own) * sea
    out[...] = forcing
    for copy in copies:
        copy.wait()
    for side, (edge, low) in enumerate(((first, 0), (last, N - HALO))):
        land_free = sea[low : low + HALO]
        for level in range(LEV - 1):
            edge[LEV + level] = m_ref[side, level] * land_free
        edge[2 * LEV - 1] = k_ref[side] * land_free
        edge[2 * LEV] = forcing[low : low + HALO]


def force(par, pieces, diag, surf, mask, *fields):
    edge = jax.ShapeDtypeStruct((2 * LEV + 1, HALO, N), f32)
    return pl.pallas_call(
        force_kernel,
        in_specs=[SMEM] + [VMEM] * 7 + [pl.BlockSpec(memory_space=pl.ANY)] * 3,
        out_specs=[VMEM, VMEM, VMEM],
        out_shape=[jax.ShapeDtypeStruct((N, N), f32), edge, edge],
        scratch_shapes=[
            pltpu.VMEM((F, 5 * UNIT + 8, N), f32),
            pltpu.VMEM((2, F, N, N), f32),
            pltpu.VMEM((2, LEV, HALO, N), f32),
            pltpu.VMEM((2, HALO, N), f32),
            pltpu.SemaphoreType.DMA((6,)),
        ],
        compiler_params=params(16),
        name="force",
    )(par, *pieces, diag, surf, mask, *fields)


def packed(get):
    lane = lax.broadcasted_iota(jnp.int32, (8, N), 1)
    first = jnp.zeros((8, N), f32)
    last = jnp.zeros((8, N), f32)
    for q, (at, width) in enumerate(PACK):
        value = get(q)
        place = (lane >= at) & (lane < at + width)
        first = jnp.where(place, pltpu.roll(value, at, 1), first)
        last = jnp.where(place, pltpu.roll(value, (at + width) % N, 1), last)
    return first, last


def column_kernel(par, state, mixing, kappa, mask, forcing, left, right, sea):
    ocean = par[0] == 1
    sea[...] = jnp.where(ocean, mask[...].astype(f32), 1.0)

    def body(t, carry):
        rows = pl.ds(pl.multiple_of(t * 8, 8), 8)
        s = sea[rows]

        def get(q):
            if q < LEV:
                return state[q, rows]
            if q < 2 * LEV - 1:
                return mixing[q - LEV, rows] * s
            if q < 2 * LEV:
                return kappa[rows] * s
            return forcing[rows]

        out = pl.ds(pl.multiple_of(HALO + t * 8, 8), 8)
        left[out], right[out] = packed(get)
        return carry

    lax.fori_loop(0, N // 8, body, 0)


def columns(par, *arrays):
    shape = jax.ShapeDtypeStruct((ROWS, N), f32)
    return pl.pallas_call(
        column_kernel,
        in_specs=[SMEM] + [VMEM] * 5,
        out_specs=[VMEM, VMEM],
        out_shape=[shape, shape],
        scratch_shapes=[pltpu.VMEM((N, N), f32)],
        compiler_params=params(16),
        cost_estimate=pl.CostEstimate(flops=2**23, bytes_accessed=2**22, transcendentals=0),
        name="columns",
    )(par, *arrays)


def corner_kernel(top, bottom, left_in, right_in, left, right):
    middle = slice(HALO, HALO + N)
    left[middle] = left_in[middle]
    right[middle] = right_in[middle]
    for halo, rows in ((top, slice(0, HALO)), (bottom, slice(HALO + N, ROWS))):
        left[rows], right[rows] = packed(lambda q, halo=halo: halo[q])


def corners(*arrays):
    shape = jax.ShapeDtypeStruct((ROWS, N), f32)
    return pl.pallas_call(
        corner_kernel,
        in_specs=[VMEM] * 4,
        out_specs=[VMEM, VMEM],
        out_shape=[shape, shape],
        compiler_params=params(16),
        name="corners",
    )(*arrays)


PAD = ROWS + 16
GROUP = 6
BLOCKS = ROWS // (8 * GROUP)
FIELDS = 2 * LEV + 1
KAP = 2 * LEV - 1
FRC = 2 * LEV
SETS = 4
SET = 32
TILES = 6
STRIP = 8 * TILES


def factors(nu, shape):
    before = ratio = None
    for level in range(LEV):
        pivot = jnp.ones(shape, f32)
        if level > 0:
            pivot = pivot + before
        if level < LEV - 1:
            here = nu(level)
            pivot = pivot + here
        if level > 0:
            pivot = pivot - before * ratio
        inverse = 1.0 / pivot
        low = before * inverse if level > 0 else None
        if level < LEV - 1:
            ratio = here * inverse
            before = here
        yield level, inverse, low, ratio if level < LEV - 1 else None


def sweep(ocean, u, at, inv, below, above, kap, frc, rows, store):
    tiles = range(len(at))
    kappa = [kap[r] for r in rows]
    keep = [1.0 - 4.0 * x for x in kappa]
    top_force = jnp.where(ocean, 1.0, 0.0)
    bottom_force = jnp.where(ocean, 0.0, 1.0)
    part = []
    for level in range(LEV):
        row = []
        for i in tiles:
            c = u[level, pl.ds(pl.multiple_of(at[i], 8), 8)]
            up = u[level, pl.ds(at[i] - 1, 8)]
            down = u[level, pl.ds(at[i] + 1, 8)]
            sides = pltpu.roll(c, 1, 1) + pltpu.roll(c, N - 1, 1)
            rhs = keep[i] * c + kappa[i] * ((up + down) + sides)
            if level == 0:
                rhs = rhs + top_force * frc[rows[i]]
            if level == LEV - 1:
                rhs = rhs + bottom_force * frc[rows[i]]
            value = rhs * inv[level, rows[i]]
            if level > 0:
                value = value + below[level, rows[i]] * part[-1][i]
            row.append(value)
        part.append(row)
    v = part[LEV - 1]
    for level in range(LEV - 1, -1, -1):
        if level < LEV - 1:
            v = [part[level][i] + above[level, rows[i]] * v[i] for i in tiles]
        for i in tiles:
            store(level, i, v[i])


def clear_ends(u, rows):
    zero = jnp.zeros((8, N), f32)
    for level in range(LEV):
        u[level, 0:8] = zero
        u[level, rows - 8 : rows] = zero


def aligned(at):
    return pl.ds(pl.multiple_of(at, 8), 8)


def inner_kernel(
    par, state, mixing, kappa, mask, top, bottom, forcing, out, strips,
    u0, ua, ub, nu, inv, below, above, kap, frc,
):
    ocean = par[0] == 1
    for u in (u0, ua, ub):
        clear_ends(u, PAD)

    def tiles(getters, rows):
        for get, at in zip(getters, rows):
            for level in range(LEV):
                u0[level, aligned(at + 8)] = get(level)
            kap[aligned(at)] = get(KAP)
            frc[aligned(at)] = get(FRC)
        steps = [factors(lambda level, get=get: get(LEV + level), (8, N)) for get in getters]
        for level in range(LEV):
            for get, at, step in zip(getters, rows, steps):
                _, inverse, low, high = next(step)
                inv[level, aligned(at)] = inverse
                if low is not None:
                    below[level, aligned(at)] = low
                if high is not None:
                    above[level, aligned(at)] = high
                    nu[level, aligned(at)] = get(LEV + level)

    tiles([lambda q: top[q], lambda q: bottom[q]], [0, HALO + N])

    def body(t, carry):
        getters, rows = [], []
        for i in range(4):
            src = aligned(t * 32 + 8 * i)
            sea = jnp.where(ocean, mask[src].astype(f32), 1.0)

            def get(q, src=src, sea=sea):
                if q < LEV:
                    return state[q, src]
                if q < KAP:
                    return mixing[q - LEV, src] * sea
                if q < FRC:
                    return kappa[src] * sea
                return forcing[src]

            getters.append(get)
            rows.append(t * 32 + 8 * i + HALO)
        tiles(getters, rows)
        return carry

    lax.fori_loop(0, N // 32, body, 0)

    lane = lax.broadcasted_iota(jnp.int32, (8, N), 1)

    def strip(j, carry):
        here = aligned(8 * j)
        for q in range(FIELDS):
            value = jnp.zeros((8, N), f32)
            for g in range(SETS):
                rows = aligned(8 * j + SET * g)
                if q < LEV:
                    c = u0[q, aligned(8 * j + SET * g + 8)]
                elif q < KAP:
                    c = nu[q - LEV, rows]
                else:
                    c = kap[rows] if q == KAP else frc[rows]
                first = SET * g
                high = (lane >= first) & (lane < first + 8)
                low = (lane >= first + 16) & (lane < first + 24)
                value = jnp.where(high, pltpu.roll(c, (first + 8) % N, 1), value)
                value = jnp.where(low, pltpu.roll(c, first + 16, 1), value)
            strips[q, here] = value
        return carry

    lax.fori_loop(0, TILES, strip, 0)

    for s in range(SWEEPS - 1):
        u, u_next = ((u0, ua), (ua, ub), (ub, ua))[s]

        def body(b, carry, u=u, u_next=u_next):
            rows = [aligned(8 * GROUP * b + 8 * i) for i in range(GROUP)]
            at = [8 * GROUP * b + 8 * i + 8 for i in range(GROUP)]

            def store(level, i, v):
                u_next[level, aligned(at[i])] = v

            sweep(ocean, u, at, inv, below, above, kap, frc, rows, store)
            return carry

        lax.fori_loop(0, BLOCKS, body, 0)

    def last(b, carry):
        base = 32 * b
        rows = [aligned(base + HALO + 8 * i) for i in range(4)]
        at = [base + HALO + 8 * i + 8 for i in range(4)]

        def store(level, i, v):
            out[level, aligned(base + 8 * i)] = v

        sweep(ocean, ua, at, inv, below, above, kap, frc, rows, store)
        return carry

    lax.fori_loop(0, N // 32, last, 0)


def inner(par, *arrays):
    wide = pltpu.VMEM((LEV, PAD, N), f32)
    rows = pltpu.VMEM((LEV, ROWS, N), f32)
    flat = pltpu.VMEM((ROWS, N), f32)
    return pl.pallas_call(
        inner_kernel,
        in_specs=[SMEM] + [VMEM] * 7,
        out_specs=[VMEM] * 2,
        out_shape=[
            jax.ShapeDtypeStruct((LEV, N, N), f32),
            jax.ShapeDtypeStruct((FIELDS, STRIP, N), f32),
        ],
        scratch_shapes=[wide] * 3 + [rows] * 4 + [flat] * 2,
        compiler_params=params(32),
        cost_estimate=pl.CostEstimate(flops=2**25, bytes_accessed=2**23, transcendentals=0),
        name="inner",
    )(par, *arrays)


def outer_kernel(
    par, inside, strips, left, right, out, sa, sb, nu, inv, below, above, kap, frc
):
    ocean = par[0] == 1
    lane = lax.broadcasted_iota(jnp.int32, (8, N), 1)
    for u in (sa, sb):
        clear_ends(u, STRIP + 16)

    def build(j, carry):
        here = aligned(8 * j)
        after, before = {}, {}
        for g in range(SETS):
            rows = aligned(8 * j + SET * g)
            after[g] = left[rows]
            before[g] = {4: pltpu.roll(right[rows], 4, 1), 3: pltpu.roll(right[rows], 5, 1)}
        for q, (at, width) in enumerate(PACK):
            value = strips[q, here]
            for g in range(SETS):
                both = jnp.where(
                    (lane >= at) & (lane < at + width),
                    after[g],
                    jnp.where((lane >= at + 8 - width) & (lane < at + 8), before[g][width], 0.0),
                )
                first = SET * g + 8
                place = (lane >= first) & (lane < first + 8)
                value = jnp.where(place, pltpu.roll(both, (first - at) % N, 1), value)
            if q < LEV:
                sa[q, aligned(8 * j + 8)] = value
            elif q < KAP:
                nu[q - LEV, here] = value
            elif q == KAP:
                kap[here] = value
            else:
                frc[here] = value
        return carry

    lax.fori_loop(0, TILES, build, 0)
    for level, inverse, low, high in factors(lambda level: nu[level], (STRIP, N)):
        inv[level] = inverse
        if low is not None:
            below[level] = low
        if high is not None:
            above[level] = high

    def pair(s, carry):
        for u, u_next in ((sa, sb), (sb, sa)):

            def store(level, i, v, u_next=u_next):
                u_next[level, 8 * i + 8 : 8 * i + 16] = v

            sweep(
                ocean, u, [8 * i + 8 for i in range(TILES)], inv, below, above, kap, frc,
                [slice(8 * i, 8 * i + 8) for i in range(TILES)], store,
            )
        return carry

    lax.fori_loop(0, SWEEPS // 2, pair, 0)

    def merge(level, carry):
        for m in range(N // 8):
            g, j = m // 4, m % 4 + 1
            edge = sa[level, 8 * j + 8 : 8 * j + 16]
            value = inside[level, 8 * m : 8 * m + 8]
            value = jnp.where(lane < 4, pltpu.roll(edge, (N - SET * g - 16) % N, 1), value)
            value = jnp.where(lane >= N - 4, pltpu.roll(edge, (N - SET * g - 8) % N, 1), value)
            out[level, 8 * m : 8 * m + 8] = value
        return carry

    lax.fori_loop(0, LEV, merge, 0)


def outer(par, *arrays):
    strip = pltpu.VMEM((LEV, STRIP + 16, N), f32)
    rows = pltpu.VMEM((LEV, STRIP, N), f32)
    flat = pltpu.VMEM((STRIP, N), f32)
    return pl.pallas_call(
        outer_kernel,
        in_specs=[SMEM] + [VMEM] * 4,
        out_specs=VMEM,
        out_shape=jax.ShapeDtypeStruct((LEV, N, N), f32),
        scratch_shapes=[strip] * 2 + [rows] * 4 + [flat] * 2,
        compiler_params=params(24),
        name="outer",
    )(par, *arrays)


def shift_pair(low_edge, high_edge, axis):
    count = lax.axis_size(axis)
    up = [(i, i + 1) for i in range(count - 1)]
    down = [(i + 1, i) for i in range(count - 1)]
    return lax.ppermute(high_edge, axis, up), lax.ppermute(low_edge, axis, down)


BOTH = ("comp", "gx")


MERGED = 16


def ocean_pairs(route):
    return [
        (GX + (2 * x + route % GX + ((x >= 8) != (route >= GX))) % GX, GX + x) for x in range(GX)
    ]


def atmosphere_pairs(route):
    return [((x + route) // 2 % GX, x) for x in range(GX) if (x + route) % 2 == 0]


def listed(block, entry):
    pairs = ocean_pairs((entry + 15) % 32) + atmosphere_pairs(entry)
    if entry == MERGED + 15:
        pairs += atmosphere_pairs(MERGED)
    return lax.ppermute(block, BOTH, pairs)


def atmosphere_routed(block, route):
    route = route % 32
    return listed(block, route if route != MERGED else MERGED + 15)


def ocean_route(units):
    base = units // 2
    odd = units % 2

    def run(peer):
        whole = (base + odd) % GX
        part = (base + 1 - odd) % GX
        half = peer[:, UNIT:] if odd else peer[:, :UNIT]
        jobs = [(peer, whole), (peer, GX + whole), (half, part), (half, GX + part)]
        entries = [(route + 17) % 32 for _, route in jobs]
        if MERGED not in entries:
            return tuple(listed(block, entry) for (block, _), entry in zip(jobs, entries))
        results = []
        last = peer[:1, :8]

        def chained(block, entry):
            nonlocal last
            block, _ = lax.optimization_barrier((block, last))
            last = listed(block, entry)
            return last

        for (block, _), entry in zip(jobs, entries):
            if entry != MERGED:
                results.append(chained(block, entry))
            else:
                low, high = chained(block, 17), chained(block, 31)
                results.append(jnp.where(lax.axis_index("gx") < 8, low, high))
        return tuple(results)

    return run


def atmosphere_route(units):
    def run(peer):
        return (
            atmosphere_routed(peer, units),
            peer,
            atmosphere_routed(peer[:, UNIT:], units - 1),
            atmosphere_routed(peer[:, :UNIT], units + 1),
        )

    return run


def shards(state, diffusivity, mixing, sea_mask, source_row, regrid_weight):
    comp = lax.axis_index("comp")
    gx = lax.axis_index("gx")
    field = state[0]
    mix = mixing[0]
    kappa = diffusivity[0]
    surf = lax.dynamic_slice(field, ((LEV - F) * (1 - comp), 0, 0), (F, N, N))
    swap = [(x, GX + x) for x in range(GX)] + [(GX + x, x) for x in range(GX)]
    peer = lax.ppermute(surf, BOTH, swap)
    where = jnp.stack([comp, gx]).astype(jnp.int32)
    source = jnp.transpose(source_row[0, :, 0, :])
    par, choice = shift(where, source)
    diag = band(regrid_weight[0])
    peer, diag = lax.optimization_barrier((peer, diag))
    pieces = lax.switch(
        choice[0],
        [atmosphere_route(i) for i in range(32)] + [ocean_route(i) for i in range(32)],
        peer,
    )
    forcing, low, high = force(par, pieces, diag, surf, sea_mask, field, mix, kappa)
    top, bottom = shift_pair(low, high, "gx")
    first, last = columns(par, field, mix, kappa, sea_mask, forcing)
    first, last = corners(top, bottom, first, last)
    before, after = shift_pair(first, last, "gy")
    inside, strips = inner(par, field, mix, kappa, sea_mask, top, bottom, forcing)
    return outer(par, inside, strips, after, before)[None]


def solution(mesh):
    placed = (
        P("comp", None, "gx", "gy"),
        P("comp", "gx", "gy"),
        P("comp", None, "gx", "gy"),
        P("gx", "gy"),
        P("comp", "gx", "gy", None),
        P("comp", "gx", None, "gy", None),
    )
    return jax.shard_map(
        shards, mesh=mesh, in_specs=placed, out_specs=P("comp", None, "gx", "gy"), check_vma=False
    )
```

```python
import functools

import jax
import jax.numpy as jnp
from jax import lax
from jax.experimental import pallas as pl
from jax.experimental.pallas import tpu as pltpu
from jax.sharding import PartitionSpec as P

F = 4
SWEEPS = 4
LEV = 16
N = 128
HALO = 8
ROWS = N + 2 * HALO
GX = 16
UNIT = 64

coupling = (0.8, 0.6, 0.4, 0.3)

f32 = jnp.float32
VMEM = pl.BlockSpec(memory_space=pltpu.VMEM)
SMEM = pl.BlockSpec(memory_space=pltpu.SMEM)

PACK = (
    [(4 * q, 4) for q in range(LEV)]
    + [(64 + 3 * i, 3) for i in range(LEV - 1)]
    + [(109, 3), (112, 3)]
)


def params(vmem_mib):
    return pltpu.CompilerParams(vmem_limit_bytes=vmem_mib * 2**20)


CHUNKS = 16


def band_kernel(comp_ref, x_ref, source, w_hbm, out_ref, par, choice, w_ref, sems):
    rows = N // CHUNKS

    def copy(i):
        at = pl.ds(i * rows, rows)
        return pltpu.make_async_copy(w_hbm.at[at], w_ref.at[at], sems.at[i])

    for i in range(CHUNKS):
        copy(i).start()
    comp, x, first = comp_ref[0], x_ref[0], source[0, 0]
    units = lax.rem(first // UNIT + 128 - jnp.where(comp == 1, 4, 1) * x, 32)
    par[0] = comp
    par[1] = x
    par[2] = lax.rem(first, UNIT)
    par[3] = units
    choice[0] = comp * 32 + units
    sub = lax.broadcasted_iota(jnp.int32, (8, N), 0)
    lane = lax.broadcasted_iota(jnp.int32, (8, N), 1)
    same = sub == lane % 8
    after = sub == (lane + 7) % 8

    def body(i, carry):
        copy(i).wait()
        base = pl.multiple_of(i * rows, rows)
        for k in range(2):
            own, nxt = [], []
            for x in range(rows):
                tile = w_ref[base + x, k, 0:8, :]
                for t in range(1, N // 8):
                    tile = tile + w_ref[base + x, k, 8 * t : 8 * t + 8, :]
                own.append(jnp.sum(jnp.where(same, tile, 0.0), axis=0, keepdims=True))
                nxt.append(jnp.sum(jnp.where(after, tile, 0.0), axis=0, keepdims=True))
            out_ref[k, pl.ds(base, rows)] = jnp.concatenate(own, axis=0)
            out_ref[2 + k, pl.ds(base, rows)] = jnp.concatenate(nxt, axis=0)
        return carry

    lax.fori_loop(0, CHUNKS, body, 0)


def band(comp, x, source, weight):
    return pl.pallas_call(
        band_kernel,
        in_specs=[SMEM, SMEM, SMEM, pl.BlockSpec(memory_space=pl.ANY)],
        out_specs=[VMEM, SMEM, SMEM],
        out_shape=[
            jax.ShapeDtypeStruct((4, N, N), f32),
            jax.ShapeDtypeStruct((4,), jnp.int32),
            jax.ShapeDtypeStruct((1,), jnp.int32),
        ],
        scratch_shapes=[pltpu.VMEM((N, 2, N, N), f32), pltpu.SemaphoreType.DMA((CHUNKS,))],
        compiler_params=params(48),
        cost_estimate=pl.CostEstimate(flops=2**22, bytes_accessed=2**24, transcendentals=0),
        name="band",
    )(comp, x, source, weight)


def force_kernel(
    par, a, b, c1, c2, diag, surf, mask, state, mixing, kappa, out, first, last,
    window, rows, m_ref, k_ref, sems,
):
    comp, x, e, units = par[0], par[1], par[2], par[3]
    copies = []
    for side, (edge, low) in enumerate(((first, 0), (last, N - HALO))):
        at = pl.ds(low, HALO)
        for n, (src, dst) in enumerate(
            (
                (state.at[:, at], edge.at[pl.ds(0, LEV)]),
                (mixing.at[:, at], m_ref.at[side]),
                (kappa.at[at], k_ref.at[side]),
            )
        ):
            copies.append(pltpu.make_async_copy(src, dst, sems.at[3 * side + n]))
    for copy in copies:
        copy.start()

    @pl.when(comp == 1)
    def _():
        odd = units % 2
        low = x < 8
        take_1 = low == (odd == 1)
        base = odd * UNIT
        at_a = pl.multiple_of(jnp.where(low, base, base + N), UNIT)
        at_b = pl.multiple_of(jnp.where(low, base + N, base), UNIT)
        at_c = pl.multiple_of((1 - odd) * 2 * N, UNIT)
        window[:, pl.ds(at_a, N), :] = a[...]
        window[:, pl.ds(at_b, N), :] = b[...]
        window[:, pl.ds(at_c, UNIT), :] = jnp.where(take_1, c1[...], c2[...])
        for f in range(F):
            for k in range(2):
                rows[k, f] = window[f, pl.ds(e + k, N, stride=2), :]

    @pl.when(comp == 0)
    def _():
        odd = (x + units) % 2

        @pl.when(odd == 0)
        def _():
            window[:, 0:N, :] = a[...]

        @pl.when(odd == 1)
        def _():
            window[:, 0:UNIT, :] = c1[...]
            window[:, UNIT:N, :] = c2[...]

        for f in range(F):
            for k in range(2):
                half = window[f, pl.ds(e + k, UNIT), :]
                rows[k, f, pl.ds(0, UNIT, stride=2), :] = half
                rows[k, f, pl.ds(1, UNIT, stride=2), :] = half

    total = jnp.zeros((N, N), f32)
    for i in range(F):
        scale = jnp.where(comp == 1, coupling[F - 1 - i], coupling[i])
        r0 = rows[0, i]
        r1 = rows[1, i]
        after = diag[2] * r0 + diag[3] * r1
        value = diag[0] * r0 + diag[1] * r1 + pltpu.roll(after, N - 1, 1)
        total = total + scale * jnp.tanh(value)
    own = surf[jnp.where(comp == 1, 0, F - 1)]
    sea = jnp.where(comp == 1, mask[...].astype(f32), 1.0)
    forcing = (total - own) * sea
    out[...] = forcing
    for copy in copies:
        copy.wait()
    for side, (edge, low) in enumerate(((first, 0), (last, N - HALO))):
        land_free = sea[low : low + HALO]
        for level in range(LEV - 1):
            edge[LEV + level] = m_ref[side, level] * land_free
        edge[2 * LEV - 1] = k_ref[side] * land_free
        edge[2 * LEV] = forcing[low : low + HALO]


def force(par, pieces, diag, surf, mask, *fields):
    edge = jax.ShapeDtypeStruct((2 * LEV + 1, HALO, N), f32)
    return pl.pallas_call(
        force_kernel,
        in_specs=[SMEM] + [VMEM] * 7 + [pl.BlockSpec(memory_space=pl.ANY)] * 3,
        out_specs=[VMEM, VMEM, VMEM],
        out_shape=[jax.ShapeDtypeStruct((N, N), f32), edge, edge],
        scratch_shapes=[
            pltpu.VMEM((F, 5 * UNIT + 8, N), f32),
            pltpu.VMEM((2, F, N, N), f32),
            pltpu.VMEM((2, LEV, HALO, N), f32),
            pltpu.VMEM((2, HALO, N), f32),
            pltpu.SemaphoreType.DMA((6,)),
        ],
        compiler_params=params(16),
        name="force",
    )(par, *pieces, diag, surf, mask, *fields)


def packed(get):
    lane = lax.broadcasted_iota(jnp.int32, (8, N), 1)
    first = jnp.zeros((8, N), f32)
    last = jnp.zeros((8, N), f32)
    for q, (at, width) in enumerate(PACK):
        value = get(q)
        place = (lane >= at) & (lane < at + width)
        first = jnp.where(place, pltpu.roll(value, at, 1), first)
        last = jnp.where(place, pltpu.roll(value, (at + width) % N, 1), last)
    return first, last


def column_kernel(par, state, mixing, kappa, mask, forcing, left, right, sea):
    ocean = par[0] == 1
    sea[...] = jnp.where(ocean, mask[...].astype(f32), 1.0)

    def body(t, carry):
        rows = pl.ds(pl.multiple_of(t * 8, 8), 8)
        s = sea[rows]

        def get(q):
            if q < LEV:
                return state[q, rows]
            if q < 2 * LEV - 1:
                return mixing[q - LEV, rows] * s
            if q < 2 * LEV:
                return kappa[rows] * s
            return forcing[rows]

        out = pl.ds(pl.multiple_of(HALO + t * 8, 8), 8)
        left[out], right[out] = packed(get)
        return carry

    lax.fori_loop(0, N // 8, body, 0, unroll=2)


def columns(par, *arrays):
    shape = jax.ShapeDtypeStruct((ROWS, N), f32)
    return pl.pallas_call(
        column_kernel,
        in_specs=[SMEM] + [VMEM] * 5,
        out_specs=[VMEM, VMEM],
        out_shape=[shape, shape],
        scratch_shapes=[pltpu.VMEM((N, N), f32)],
        compiler_params=params(16),
        cost_estimate=pl.CostEstimate(flops=2**23, bytes_accessed=2**22, transcendentals=0),
        name="columns",
    )(par, *arrays)


def corner_kernel(top, bottom, left_in, right_in, left, right):
    middle = slice(HALO, HALO + N)
    left[middle] = left_in[middle]
    right[middle] = right_in[middle]
    for halo, rows in ((top, slice(0, HALO)), (bottom, slice(HALO + N, ROWS))):
        left[rows], right[rows] = packed(lambda q, halo=halo: halo[q])


def corners(*arrays):
    shape = jax.ShapeDtypeStruct((ROWS, N), f32)
    return pl.pallas_call(
        corner_kernel,
        in_specs=[VMEM] * 4,
        out_specs=[VMEM, VMEM],
        out_shape=[shape, shape],
        compiler_params=params(16),
        name="corners",
    )(*arrays)


PAD = ROWS + 16
GROUP = 6
BLOCKS = ROWS // (8 * GROUP)
FIELDS = 2 * LEV + 1
KAP = 2 * LEV - 1
FRC = 2 * LEV
SETS = 4
SET = 32
TILES = 6
STRIP = 8 * TILES


def factors(nu, shape):
    before = ratio = None
    for level in range(LEV):
        pivot = jnp.ones(shape, f32)
        if level > 0:
            pivot = pivot + before
        if level < LEV - 1:
            here = nu(level)
            pivot = pivot + here
        if level > 0:
            pivot = pivot - before * ratio
        inverse = 1.0 / pivot
        low = before * inverse if level > 0 else None
        if level < LEV - 1:
            ratio = here * inverse
            before = here
        yield level, inverse, low, ratio if level < LEV - 1 else None


def sweep(ocean, u, at, inv, below, above, kap, frc, rows, store):
    tiles = range(len(at))
    kappa = [kap[r] for r in rows]
    keep = [1.0 - 4.0 * x for x in kappa]
    top_force = jnp.where(ocean, 1.0, 0.0)
    bottom_force = jnp.where(ocean, 0.0, 1.0)
    part = []
    for level in range(LEV):
        row = []
        for i in tiles:
            c = u[level, pl.ds(pl.multiple_of(at[i], 8), 8)]
            up = u[level, pl.ds(at[i] - 1, 8)]
            down = u[level, pl.ds(at[i] + 1, 8)]
            sides = pltpu.roll(c, 1, 1) + pltpu.roll(c, N - 1, 1)
            rhs = keep[i] * c + kappa[i] * ((up + down) + sides)
            if level == 0:
                rhs = rhs + top_force * frc[rows[i]]
            if level == LEV - 1:
                rhs = rhs + bottom_force * frc[rows[i]]
            value = rhs * inv[level, rows[i]]
            if level > 0:
                value = value + below[level, rows[i]] * part[-1][i]
            row.append(value)
        part.append(row)
    v = part[LEV - 1]
    for level in range(LEV - 1, -1, -1):
        if level < LEV - 1:
            v = [part[level][i] + above[level, rows[i]] * v[i] for i in tiles]
        for i in tiles:
            store(level, i, v[i])


def clear_ends(u, rows):
    zero = jnp.zeros((8, N), f32)
    for level in range(LEV):
        u[level, 0:8] = zero
        u[level, rows - 8 : rows] = zero


def aligned(at):
    return pl.ds(pl.multiple_of(at, 8), 8)


def inner_kernel(
    par, state, mixing, kappa, mask, top, bottom, forcing, out, strips,
    u0, ua, ub, nu, inv, below, above, kap, frc,
):
    ocean = par[0] == 1
    for u in (u0, ua, ub):
        clear_ends(u, PAD)

    def tiles(getters, rows):
        for get, at in zip(getters, rows):
            for level in range(LEV):
                u0[level, aligned(at + 8)] = get(level)
            kap[aligned(at)] = get(KAP)
            frc[aligned(at)] = get(FRC)
        steps = [factors(lambda level, get=get: get(LEV + level), (8, N)) for get in getters]
        for level in range(LEV):
            for get, at, step in zip(getters, rows, steps):
                _, inverse, low, high = next(step)
                inv[level, aligned(at)] = inverse
                if low is not None:
                    below[level, aligned(at)] = low
                if high is not None:
                    above[level, aligned(at)] = high
                    nu[level, aligned(at)] = get(LEV + level)

    tiles([lambda q: top[q], lambda q: bottom[q]], [0, HALO + N])

    def body(t, carry):
        getters, rows = [], []
        for i in range(4):
            src = aligned(t * 32 + 8 * i)
            sea = jnp.where(ocean, mask[src].astype(f32), 1.0)

            def get(q, src=src, sea=sea):
                if q < LEV:
                    return state[q, src]
                if q < KAP:
                    return mixing[q - LEV, src] * sea
                if q < FRC:
                    return kappa[src] * sea
                return forcing[src]

            getters.append(get)
            rows.append(t * 32 + 8 * i + HALO)
        tiles(getters, rows)
        return carry

    lax.fori_loop(0, N // 32, body, 0)

    lane = lax.broadcasted_iota(jnp.int32, (8, N), 1)

    def strip(j, carry):
        here = aligned(8 * j)
        for q in range(FIELDS):
            value = jnp.zeros((8, N), f32)
            for g in range(SETS):
                rows = aligned(8 * j + SET * g)
                if q < LEV:
                    c = u0[q, aligned(8 * j + SET * g + 8)]
                elif q < KAP:
                    c = nu[q - LEV, rows]
                else:
                    c = kap[rows] if q == KAP else frc[rows]
                first = SET * g
                high = (lane >= first) & (lane < first + 8)
                low = (lane >= first + 16) & (lane < first + 24)
                value = jnp.where(high, pltpu.roll(c, (first + 8) % N, 1), value)
                value = jnp.where(low, pltpu.roll(c, first + 16, 1), value)
            strips[q, here] = value
        return carry

    lax.fori_loop(0, TILES, strip, 0, unroll=2)

    for s in range(SWEEPS - 1):
        u, u_next = ((u0, ua), (ua, ub), (ub, ua))[s]

        def body(b, carry, u=u, u_next=u_next):
            rows = [aligned(8 * GROUP * b + 8 * i) for i in range(GROUP)]
            at = [8 * GROUP * b + 8 * i + 8 for i in range(GROUP)]

            def store(level, i, v):
                u_next[level, aligned(at[i])] = v

            sweep(ocean, u, at, inv, below, above, kap, frc, rows, store)
            return carry

        lax.fori_loop(0, BLOCKS, body, 0)

    def last(b, carry):
        base = 32 * b
        rows = [aligned(base + HALO + 8 * i) for i in range(4)]
        at = [base + HALO + 8 * i + 8 for i in range(4)]

        def store(level, i, v):
            out[level, aligned(base + 8 * i)] = v

        sweep(ocean, ua, at, inv, below, above, kap, frc, rows, store)
        return carry

    lax.fori_loop(0, N // 32, last, 0)


def inner(par, *arrays):
    wide = pltpu.VMEM((LEV, PAD, N), f32)
    rows = pltpu.VMEM((LEV, ROWS, N), f32)
    flat = pltpu.VMEM((ROWS, N), f32)
    return pl.pallas_call(
        inner_kernel,
        in_specs=[SMEM] + [VMEM] * 7,
        out_specs=[VMEM] * 2,
        out_shape=[
            jax.ShapeDtypeStruct((LEV, N, N), f32),
            jax.ShapeDtypeStruct((FIELDS, STRIP, N), f32),
        ],
        scratch_shapes=[wide] * 3 + [rows] * 4 + [flat] * 2,
        compiler_params=params(32),
        cost_estimate=pl.CostEstimate(flops=2**25, bytes_accessed=2**23, transcendentals=0),
        name="inner",
    )(par, *arrays)


def outer_kernel(
    par, inside, strips, left, right, out, sa, sb, nu, inv, below, above, kap, frc, whole, sems
):
    ocean = par[0] == 1
    lane = lax.broadcasted_iota(jnp.int32, (8, N), 1)
    for u in (sa, sb):
        clear_ends(u, STRIP + 16)

    masks = {}
    for width, start in ((4, 0), (3, 4 * LEV)):
        stride = 8 if width == 4 else 9
        for c in range(stride // width):
            phase = (lane + 9 * N - start - width * c) % stride
            masks[width, c] = (phase < width, (phase >= 8 - width) & (phase < 8))
    place = [(lane >= SET * g + 8) & (lane < SET * g + 16) for g in range(SETS)]
    upper = (lane & (SET - 1)) < 8
    outside = (lane < 4) | (lane >= N - 4)

    def build(j, carry):
        here = aligned(8 * j)
        merged = []
        for g in range(SETS):
            rows = aligned(8 * j + SET * g)
            after = left[rows]
            before = {4: pltpu.roll(right[rows], 4, 1), 3: pltpu.roll(right[rows], 5, 1)}
            pieces = {
                key: jnp.where(one, after, jnp.where(two, before[key[0]], 0.0))
                for key, (one, two) in masks.items()
            }
            merged.append(pieces)
        for q, (at, width) in enumerate(PACK):
            value = strips[q, here]
            c = q % 2 if width == 4 else (at - 4 * LEV) // 3 % 3
            for g in range(SETS):
                first = SET * g + 8
                value = jnp.where(place[g], pltpu.roll(merged[g][width, c], (first - at) % N, 1), value)
            if q < LEV:
                sa[q, aligned(8 * j + 8)] = value
            elif q < KAP:
                nu[q - LEV, here] = value
            elif q == KAP:
                kap[here] = value
            else:
                frc[here] = value
        return carry

    lax.fori_loop(0, TILES, build, 0, unroll=2)
    for level, inverse, low, high in factors(lambda level: nu[level], (STRIP, N)):
        inv[level] = inverse
        if low is not None:
            below[level] = low
        if high is not None:
            above[level] = high

    def pair(s, carry):
        for u, u_next in ((sa, sb), (sb, sa)):

            def store(level, i, v, u_next=u_next):
                u_next[level, 8 * i + 8 : 8 * i + 16] = v

            sweep(
                ocean, u, [8 * i + 8 for i in range(TILES)], inv, below, above, kap, frc,
                [slice(8 * i, 8 * i + 8) for i in range(TILES)], store,
            )
        return carry

    lax.fori_loop(0, SWEEPS // 2, pair, 0)

    def copy(part):
        levels = pl.ds(4 * part, 4)
        return pltpu.make_async_copy(whole.at[levels], out.at[levels], sems.at[part])

    def merge(part, carry):
        for level in range(4):
            level = 4 * part + level
            for j in range(1, TILES - 1):
                edge = sa[level, 8 * j + 8 : 8 * j + 16]
                edge = jnp.where(upper, edge, pltpu.roll(edge, N - 8, 1))
                for g in range(SETS):
                    m = 4 * g + j - 1
                    moved = pltpu.roll(edge, (N - SET * g - 8) % N, 1)
                    own = inside[level, 8 * m : 8 * m + 8]
                    whole[level, 8 * m : 8 * m + 8] = jnp.where(outside, moved, own)
        copy(part).start()
        return carry

    lax.fori_loop(0, LEV // 4, merge, 0)
    for part in range(LEV // 4):
        copy(part).wait()


def outer(par, *arrays):
    strip = pltpu.VMEM((LEV, STRIP + 16, N), f32)
    rows = pltpu.VMEM((LEV, STRIP, N), f32)
    flat = pltpu.VMEM((STRIP, N), f32)
    return pl.pallas_call(
        outer_kernel,
        in_specs=[SMEM] + [VMEM] * 4,
        out_specs=pl.BlockSpec(memory_space=pl.ANY),
        out_shape=jax.ShapeDtypeStruct((LEV, N, N), f32),
        scratch_shapes=[strip] * 2
        + [rows] * 4
        + [flat] * 2
        + [pltpu.VMEM((LEV, N, N), f32), pltpu.SemaphoreType.DMA((LEV // 4,))],
        compiler_params=params(24),
        name="outer",
    )(par, *arrays)


def shift_pair(low_edge, high_edge, axis):
    count = lax.axis_size(axis)
    up = [(i, i + 1) for i in range(count - 1)]
    down = [(i + 1, i) for i in range(count - 1)]
    return lax.ppermute(high_edge, axis, up), lax.ppermute(low_edge, axis, down)


BOTH = ("comp", "gx")


MERGED = 16


def ocean_pairs(route):
    return [
        (GX + (2 * x + route % GX + ((x >= 8) != (route >= GX))) % GX, GX + x) for x in range(GX)
    ]


def atmosphere_pairs(route):
    return [((x + route) // 2 % GX, x) for x in range(GX) if (x + route) % 2 == 0]


def listed(block, entry):
    pairs = ocean_pairs((entry + 15) % 32) + atmosphere_pairs(entry)
    if entry == MERGED + 15:
        pairs += atmosphere_pairs(MERGED)
    return lax.ppermute(block, BOTH, pairs)


def atmosphere_routed(block, route):
    route = route % 32
    return listed(block, route if route != MERGED else MERGED + 15)


def ocean_route(units):
    base = units // 2
    odd = units % 2

    def run(peer):
        whole = (base + odd) % GX
        part = (base + 1 - odd) % GX
        half = peer[:, UNIT:] if odd else peer[:, :UNIT]
        jobs = [(peer, whole), (peer, GX + whole), (half, part), (half, GX + part)]
        entries = [(route + 17) % 32 for _, route in jobs]
        if MERGED not in entries:
            return tuple(listed(block, entry) for (block, _), entry in zip(jobs, entries))
        results = []
        last = peer[:1, :8]

        def chained(block, entry):
            nonlocal last
            block, _ = lax.optimization_barrier((block, last))
            last = listed(block, entry)
            return last

        for (block, _), entry in zip(jobs, entries):
            if entry != MERGED:
                results.append(chained(block, entry))
            else:
                low, high = chained(block, 17), chained(block, 31)
                results.append(jnp.where(lax.axis_index("gx") < 8, low, high))
        return tuple(results)

    return run


def atmosphere_route(units):
    def run(peer):
        return (
            atmosphere_routed(peer, units),
            peer,
            atmosphere_routed(peer[:, UNIT:], units - 1),
            atmosphere_routed(peer[:, :UNIT], units + 1),
        )

    return run


def shards(state, diffusivity, mixing, sea_mask, source_row, regrid_weight):
    comp = lax.axis_index("comp")
    gx = lax.axis_index("gx")
    field = state[0]
    mix = mixing[0]
    kappa = diffusivity[0]
    surf = lax.dynamic_slice(field, ((LEV - F) * (1 - comp), 0, 0), (F, N, N))
    swap = [(x, GX + x) for x in range(GX)] + [(GX + x, x) for x in range(GX)]
    peer = lax.ppermute(surf, BOTH, swap)
    source = jnp.transpose(source_row[0, :, 0, :])
    diag, par, choice = band(
        jnp.reshape(comp, (1,)), jnp.reshape(gx, (1,)), source, regrid_weight[0]
    )
    peer, diag = lax.optimization_barrier((peer, diag))
    pieces = lax.switch(
        choice[0],
        [atmosphere_route(i) for i in range(32)] + [ocean_route(i) for i in range(32)],
        peer,
    )
    forcing, low, high = force(par, pieces, diag, surf, sea_mask, field, mix, kappa)
    top, bottom = shift_pair(low, high, "gx")
    first, last = columns(par, field, mix, kappa, sea_mask, forcing)
    first, last = corners(top, bottom, first, last)
    before, after = shift_pair(first, last, "gy")
    inside, strips = inner(par, field, mix, kappa, sea_mask, top, bottom, forcing)
    return outer(par, inside, strips, after, before)[None]


def solution(mesh):
    placed = (
        P("comp", None, "gx", "gy"),
        P("comp", "gx", "gy"),
        P("comp", None, "gx", "gy"),
        P("gx", "gy"),
        P("comp", "gx", "gy", None),
        P("comp", "gx", None, "gy", None),
    )
    return jax.shard_map(
        shards, mesh=mesh, in_specs=placed, out_specs=P("comp", None, "gx", "gy"), check_vma=False
    )
```
